32 devices in a mesh: groups: 2 (over y), dap: 4 (over z), chan: 2 (over x), sub: 2 (over core).
Axes of the slice: x: 2, y: 2, z: 4, core: 2. Of those that a mesh axis runs over, the one named last changes fastest.
Arguments:
- pair: bfloat16 [96, 48, 128], P(('groups', 'dap'), ('chan', 'sub')), parts along dimension 0, may hold values from -6 to 6
- cotangent: bfloat16 [96, 48, 128], P(('groups', 'dap'), ('chan', 'sub')), parts along dimension 0, may hold values from -6 to 6
- mask: int32 [96], P('groups'), parts along dimension 0, may hold values 0 or 1
- norm_gain: float32 [128], replicated, may hold values from 0.1 to 1.9
- norm_bias: float32 [128], replicated, may hold values from -2.5 to 2.5
- w_proj: bfloat16 [128, 512], replicated, may hold values from -0.5 to 0.5
- w_gate: bfloat16 [128, 128], replicated, may hold values from -0.5 to 0.5
- output_norm_gain: float32 [128], replicated, may hold values from 0.1 to 1.9
- output_norm_bias: float32 [128], replicated, may hold values from -2.5 to 2.5
- w_out: bfloat16 [128, 128], replicated, may hold values from -0.5 to 0.5
Outputs:
- update: bfloat16 [96, 48, 128], P(('groups', 'dap'), ('chan', 'sub')), parts along dimension 0
- grad_pair: bfloat16 [96, 48, 128], P(('groups', 'dap'), ('chan', 'sub')), parts along dimension 0
- grad_proj: float32 [256, 512], P('groups'), parts along dimension 0
The draws below stay inside these ranges and needn't reach their ends.
There are 2 independent parts, one for each index of `groups`. The reference program is written for one: setup_inputs(seed, part) draws one part's arguments, and reference() takes and returns one part's arrays. A program takes and returns all parts, laid end to end along the dimension named above; an argument that names none is the same for every part. Nothing has to cross between parts.
All inputs are finite; a program needn't handle non-finite values.
Results may differ from the reference program's by a relative error of at most 0.0095.
Values may be sent and summed in bfloat16 or wider, within the bound.
A program may use at most 64 MiB of HBM per device.

```python
import jax
import jax.numpy as jnp
from jax import lax

C = 128
H = 128
N = 48


def place_ends(result, stream_key, least, largest):
    shape = result.shape
    index_at = [jax.random.randint(jax.random.fold_in(stream_key, axis), (), 0, shape[axis]) for axis in range(len(shape))]
    result = result.at[tuple(index_at)].set(least)
    longest = shape.index(max(shape))
    index_at[longest] = (index_at[longest] + 1) % shape[longest]
    return result.at[tuple(index_at)].set(largest)


def block_levels(key, shape, cuts, least, largest):
    def one(position, parts):
        draws = jax.random.uniform(jax.random.fold_in(jax.random.fold_in(key, 6), position), (parts,), jnp.float32, least / len(cuts), largest / len(cuts))
        return jnp.repeat(jnp.exp(draws), shape[position] // parts).reshape((-1,) + (1,) * (len(shape) - position - 1))

    level = one(*cuts[0])
    for cut in cuts[1:]:
        level = level * one(*cut)
    return level


def normal_values(own_key, shape, spread, limit, shards=(), kind=jnp.bfloat16):
    drawn = spread * jax.random.normal(own_key, shape, jnp.float32)
    if shards:
        drawn = drawn * block_levels(own_key, shape, shards, -0.22, 0.18)
    return jnp.clip(drawn, -limit, limit).astype(kind)


def setup_inputs(seed: int = 0, part: int = 0) -> dict:
    streams_of = jax.random.split(jax.random.key(seed), 11)
    own_keys = jax.random.split(jax.random.fold_in(streams_of[10], part), 11)
    pair = normal_values(own_keys[0], (N, N, C), 1.0, 6.0, ((0, 4), (1, 4)))
    cotangent = normal_values(own_keys[1], (N, N, C), 1.0, 6.0, ((0, 4), (1, 4)))
    mask = place_ends((jax.random.randint(own_keys[2], (N,), 0, 8) < 7).astype(jnp.int32), jax.random.fold_in(own_keys[2], 1), 0, 1)
    norm_gain = jnp.clip(1.0 + 0.18 * jax.random.normal(streams_of[3], (C,), jnp.float32), 0.1, 1.9)
    norm_bias = normal_values(streams_of[4], (C,), 0.5, 2.5, (), jnp.float32)
    w_proj = normal_values(streams_of[5], (C, 4 * H), C ** -0.5, 0.5)
    w_gate = normal_values(streams_of[6], (C, C), C ** -0.5, 0.5)
    output_norm_gain = jnp.clip(1.0 + 0.18 * jax.random.normal(streams_of[7], (H,), jnp.float32), 0.1, 1.9)
    output_norm_bias = normal_values(streams_of[8], (H,), 0.5, 2.5, (), jnp.float32)
    w_out = normal_values(streams_of[9], (H, C), H ** -0.5, 0.5)
    return dict(pair=pair, cotangent=cotangent, mask=mask, norm_gain=norm_gain, norm_bias=norm_bias, w_proj=w_proj, w_gate=w_gate, output_norm_gain=output_norm_gain, output_norm_bias=output_norm_bias, w_out=w_out)


def layer_normalize(value, gain, bias):
    mean = lax.optimization_barrier(jnp.mean(value, axis=-1, keepdims=True))
    centred = value - mean
    inverse = 1.0 / jnp.sqrt(lax.optimization_barrier(jnp.mean(centred * centred, axis=-1, keepdims=True)) + 1e-05)
    normal = centred * inverse
    return (normal * gain + bias, normal, inverse)

def norm_backward_pass(incoming, normal, inverse, gain):
    scaled = incoming * gain
    return inverse * (scaled - lax.optimization_barrier(jnp.mean(scaled, axis=-1, keepdims=True)) - normal * lax.optimization_barrier(jnp.mean(scaled * normal, axis=-1, keepdims=True)))

def reference(pair, cotangent, mask, norm_gain, norm_bias, w_proj, w_gate, output_norm_gain, output_norm_bias, w_out):
    normed_f, zhat, zinv = layer_normalize(pair.astype(jnp.float32), norm_gain, norm_bias)
    normed = normed_f.astype(jnp.bfloat16)
    proj = jnp.einsum('ikc,cq->ikq', normed, w_proj, preferred_element_type=jnp.float32)
    left_val, left_gate, right_val, right_gate = jnp.split(proj, 4, axis=2)
    maskf = mask.astype(jnp.float32)
    pmask = (maskf[:, None] * maskf[None, :])[:, :, None]
    left_sig = jax.nn.sigmoid(left_gate)
    right_sig = jax.nn.sigmoid(right_gate)
    left = (pmask * left_sig * left_val).astype(jnp.bfloat16)
    right = (pmask * right_sig * right_val).astype(jnp.bfloat16)
    left_f = left.astype(jnp.float32)
    right_f = right.astype(jnp.float32)
    mixed_product = jnp.einsum('ikh,jkh->ijh', left_f, right_f).astype(jnp.bfloat16)
    mixed_product_float, centred_scaled_input, inverse_deviation = layer_normalize(mixed_product.astype(jnp.float32), output_norm_gain, output_norm_bias)
    mixed_norm = mixed_product_float.astype(jnp.bfloat16)
    value = jnp.einsum('ijh,hc->ijc', mixed_norm, w_out, preferred_element_type=jnp.float32)
    gate = jax.nn.sigmoid(jnp.einsum('ijc,cd->ijd', normed, w_gate, preferred_element_type=jnp.float32))
    update = (gate * value).astype(jnp.bfloat16)
    upstream = cotangent.astype(jnp.float32)
    d_value = (upstream * gate).astype(jnp.bfloat16)
    d_gate = (upstream * value * gate * (1.0 - gate)).astype(jnp.bfloat16)
    norm_gradient = jnp.einsum('ijc,hc->ijh', d_value, w_out, preferred_element_type=jnp.float32)
    mixed_gradient = norm_backward_pass(norm_gradient, centred_scaled_input, inverse_deviation, output_norm_gain).astype(jnp.bfloat16)
    d_mixed_f = mixed_gradient.astype(jnp.float32)
    d_left = jnp.einsum('ijh,jkh->ikh', d_mixed_f, right_f).astype(jnp.float32)
    d_right = jnp.einsum('ijh,ikh->jkh', d_mixed_f, left_f)
    d_left = d_left.astype(jnp.bfloat16).astype(jnp.float32)
    d_right = d_right.astype(jnp.bfloat16).astype(jnp.float32)
    d_proj = jnp.concatenate([pmask * left_sig * d_left, pmask * left_val * left_sig * (1.0 - left_sig) * d_left, pmask * right_sig * d_right, pmask * right_val * right_sig * (1.0 - right_sig) * d_right], axis=2).astype(jnp.bfloat16)
    d_normed = jnp.einsum('ikq,cq->ikc', d_proj, w_proj, preferred_element_type=jnp.float32)
    d_normed = d_normed + jnp.einsum('ikd,cd->ikc', d_gate, w_gate, preferred_element_type=jnp.float32)
    grad_pair = norm_backward_pass(d_normed, zhat, zinv, norm_gain).astype(jnp.bfloat16)
    grad_proj = jnp.einsum('ikc,ikq->cq', normed, d_proj, preferred_element_type=jnp.float32)
    return (update, grad_pair, grad_proj)
```

```python
import functools

import jax
import jax.numpy as jnp
from jax import lax
from jax.experimental import pallas as pl
from jax.experimental.pallas import tpu as pltpu
from jax.sharding import PartitionSpec as P

MESH = pl.DeviceIdType.MESH
F32 = jnp.float32
BF16 = jnp.bfloat16


def nn(a, b):
    return jnp.dot(a, b, preferred_element_type=F32)


def nt(a, b):
    return lax.dot_general(a, b, (((1,), (1,)), ((), ())), preferred_element_type=F32)


def tn(a, b):
    return lax.dot_general(a, b, (((0,), (0,)), ((), ())), preferred_element_type=F32)


def normalize(value):
    mean = jnp.mean(value, axis=1, keepdims=True)
    centred = value - mean
    inverse = lax.rsqrt(jnp.mean(centred * centred, axis=1, keepdims=True) + 1e-05)
    return centred * inverse, inverse


def norm_backward(incoming, normal, inverse, gain):
    scaled = incoming * gain
    return inverse * (
        scaled
        - jnp.mean(scaled, axis=1, keepdims=True)
        - normal * jnp.mean(scaled * normal, axis=1, keepdims=True)
    )


def kernel(
    dims,
    pair_ref,
    cot_ref,
    mask_ref,
    ng_ref,
    nb_ref,
    wp_ref,
    wg_ref,
    og_ref,
    ob_ref,
    wo_ref,
    update_ref,
    gpair_ref,
    gproj_ref,
    flat,
    flat2,
    left_in,
    right_in,
    left_own,
    right_own,
    left_all,
    right_all,
    cube,
    dm_row,
    dm_col,
    dl_all,
    dr_all,
    stage,
    dl_out,
    dr_out,
    dl_in,
    dr_in,
    g1_out,
    g1_in,
    g2_in,
    g3_in,
    s_right,
    s_left,
    s_dr,
    s_dl,
    s_g1,
    s_g2,
    s_g3,
    r_right,
    r_left,
    r_dr,
    r_dl,
    r_g1,
    r_g2,
    r_g3,
):
    R, K, D, G, nsub = dims
    N = K * G
    M = R * K
    T = K // R
    d = lax.axis_index("dap")
    c = lax.axis_index("chan") * nsub + lax.axis_index("sub")

    def at(dd, cc):
        return {"dap": dd, "chan": lax.div(cc, nsub), "sub": lax.rem(cc, nsub)}

    def copy(src, dst, send, recv, dd, cc):
        return pltpu.make_async_remote_copy(
            src_ref=src, dst_ref=dst, send_sem=send, recv_sem=recv,
            device_id=at(dd, cc), device_id_type=MESH,
        )

    barrier = pltpu.get_barrier_semaphore()
    me = d * G + c

    def greet(step, carry):
        other = lax.rem(me + step, D * G)
        pl.semaphore_signal(
            barrier, inc=1, device_id=at(lax.div(other, G), lax.rem(other, G)), device_id_type=MESH
        )
        return carry

    lax.fori_loop(1, D * G, greet, 0)

    for i in range(R):
        flat[i * K : (i + 1) * K] = pair_ref[i].astype(F32)
        flat2[i * K : (i + 1) * K] = cot_ref[i].astype(F32)
    zhat, zinv = normalize(flat[...])
    normed = (zhat * ng_ref[...] + nb_ref[...]).astype(BF16)
    row_at = lax.broadcasted_iota(jnp.int32, (M, N), 0)
    lane_at = lax.broadcasted_iota(jnp.int32, (M, N), 1)
    row_i = lax.div(row_at, K)
    row_k = row_at - row_i * K
    maskf = jnp.broadcast_to(mask_ref[...].astype(F32), (M, N))
    row_mask = jnp.sum(jnp.where(lane_at == row_i + d * R, maskf, 0.0), axis=1, keepdims=True)
    col_mask = jnp.sum(jnp.where(lane_at == row_k + c * K, maskf, 0.0), axis=1, keepdims=True)
    pmask = row_mask * col_mask

    right_val = nn(normed, wp_ref[:, 256:384])
    right_sig = jax.nn.sigmoid(nn(normed, wp_ref[:, 384:512]))
    right_own[...] = (pmask * right_sig * right_val).astype(BF16)
    home = lax.div(d, T)
    part = lax.rem(d, T)
    pl.semaphore_wait(barrier, D * G - 1)

    def send_right(step):
        to = lax.rem(d + step, D)
        return copy(
            right_own, right_in.at[part * G + c], s_right.at[step], r_right.at[part * G + c], to, home
        )

    for step in range(1, D):
        send_right(step).start()

    @pl.when(c != home)
    def _():
        send_right(0).start()

    @pl.when(c == home)
    def _():
        right_in[part * G + c] = right_own[...]

    left_val = nn(normed, wp_ref[:, 0:128])
    left_sig = jax.nn.sigmoid(nn(normed, wp_ref[:, 128:256]))
    left_own[...] = (pmask * left_sig * left_val).astype(BF16)

    def send_left(step):
        to = lax.rem(c + step, G)
        return copy(left_own, left_in.at[c], s_left.at[step], r_left.at[c], d, to)

    for step in range(1, G):
        send_left(step).start()
    left_in[c] = left_own[...]
    gate = jax.nn.sigmoid(nn(normed, wg_ref[...]))

    def get_left(step):
        frm = lax.rem(c + step, G)
        return copy(left_own, left_in.at[frm], s_left.at[step], r_left.at[frm], d, frm)

    for step in range(1, G):
        get_left(step).wait_recv()
    for k in range(G):
        flat[...] = left_in[k].astype(F32)
        for i in range(R):
            left_all[i, k * K : (k + 1) * K] = flat[i * K : (i + 1) * K]

    for t in range(T):
        for k in range(G):
            slot = t * G + k

            @pl.when(jnp.logical_or(c * T + t != d, c != k))
            def _(slot=slot, t=t, k=k):
                copy(
                    right_own, right_in.at[slot], s_right.at[0], r_right.at[slot], c * T + t, k
                ).wait_recv()

    for t in range(T):
        for k in range(G):
            stage[...] = right_in[t * G + k].astype(F32)
            for i in range(R):
                right_all[t * R + i, k * K : (k + 1) * K] = stage[i * K : (i + 1) * K]

    def mix_row(i, carry):
        row = left_all[i]
        for t in range(T):
            cube[i, t * R : (t + 1) * R] = jnp.sum(
                row[None] * right_all[t * R : (t + 1) * R], axis=1
            )
        return carry

    lax.fori_loop(0, R, mix_row, 0)
    for i in range(R):
        flat[i * K : (i + 1) * K] = cube[i]
    vhat, vinv = normalize(flat[...].astype(BF16).astype(F32))
    mixed_norm = (vhat * og_ref[...] + ob_ref[...]).astype(BF16)
    value = nn(mixed_norm, wo_ref[...])
    upstream = flat2[...]
    d_value = (upstream * gate).astype(BF16)
    d_mixed = norm_backward(nt(d_value, wo_ref[...]), vhat, vinv, og_ref[...])
    flat[...] = d_mixed.astype(BF16).astype(F32)
    for i in range(R):
        dm_row[i] = flat[i * K : (i + 1) * K]
    for j in range(K):
        dm_col[j] = flat[pl.ds(j, R, stride=K)]

    chunk = 48 if N % 48 == 0 else N

    def dr_row(j, carry):
        weights = dm_col[j]
        for s in range(N // chunk):
            total = None
            for i in range(R):
                term = weights[i : i + 1] * left_all[i, s * chunk : (s + 1) * chunk]
                total = term if total is None else total + term
            dr_all[j, s * chunk : (s + 1) * chunk] = total
        return carry

    lax.fori_loop(0, K, dr_row, 0)

    def send_dr(t, k):
        slot = t * G + k
        return copy(dr_out.at[slot], dr_in.at[d], s_dr.at[slot], r_dr.at[d], c * T + t, k)

    for t in range(T):
        for k in range(G):
            slot = t * G + k
            for i in range(R):
                stage[i * K : (i + 1) * K] = dr_all[t * R + i, k * K : (k + 1) * K]
            dr_out[slot] = stage[...].astype(BF16)
            mine = jnp.logical_and(c * T + t == d, c == k)

            @pl.when(jnp.logical_not(mine))
            def _(t=t, k=k):
                send_dr(t, k).start()

            @pl.when(mine)
            def _(slot=slot):
                dr_in[d] = dr_out[slot]

    def dl_row(i, carry):
        weights = dm_row[i]
        for s in range(N // chunk):
            total = None
            for j in range(K):
                term = weights[j : j + 1] * right_all[j, s * chunk : (s + 1) * chunk]
                total = term if total is None else total + term
            dl_all[i, s * chunk : (s + 1) * chunk] = total
        return carry

    lax.fori_loop(0, R, dl_row, 0)

    def send_dl(k):
        return copy(dl_out.at[k], dl_in.at[c], s_dl.at[k], r_dl.at[c], d, k)

    for k in range(G):
        for i in range(R):
            stage[i * K : (i + 1) * K] = dl_all[i, k * K : (k + 1) * K]
        dl_out[k] = stage[...].astype(BF16)

        @pl.when(c != k)
        def _(k=k):
            send_dl(k).start()

        @pl.when(c == k)
        def _(k=k):
            dl_in[c] = dl_out[k]

    flat[...] = gate * value
    for i in range(R):
        update_ref[i] = flat[i * K : (i + 1) * K].astype(BF16)
    d_gate = (upstream * value * gate * (1.0 - gate)).astype(BF16)
    d_normed = nt(d_gate, wg_ref[...])
    left_scale = pmask * left_sig
    left_scale2 = left_scale * left_val * (1.0 - left_sig)
    right_scale = pmask * right_sig
    right_scale2 = right_scale * right_val * (1.0 - right_sig)

    for k in range(G):

        @pl.when(c != k)
        def _(k=k):
            copy(dl_out.at[k], dl_in.at[k], s_dl.at[k], r_dl.at[k], d, k).wait_recv()

    d_left = dl_in[0].astype(F32)
    for k in range(1, G):
        d_left = d_left + dl_in[k].astype(F32)
    dp0 = (left_scale * d_left).astype(BF16)
    dp1 = (left_scale2 * d_left).astype(BF16)
    S = 128 // G
    grads = [tn(normed, dp0), tn(normed, dp1)]

    for k in range(D):

        @pl.when(jnp.logical_or(c != home, d != k))
        def _(k=k):
            copy(dr_out.at[0], dr_in.at[k], s_dr.at[0], r_dr.at[k], k, home).wait_recv()

    d_right = dr_in[0].astype(F32)
    for k in range(1, D):
        d_right = d_right + dr_in[k].astype(F32)
    dp2 = (right_scale * d_right).astype(BF16)
    dp3 = (right_scale2 * d_right).astype(BF16)
    grads += [tn(normed, dp2), tn(normed, dp3)]
    for q in range(4):
        for k in range(G):
            g1_out[k, :, q * 128 : (q + 1) * 128] = grads[q][k * S : (k + 1) * S].astype(BF16)

    def send_g1(k):
        return copy(g1_out.at[k], g1_in.at[c], s_g1.at[k], r_g1.at[c], d, k)

    for k in range(G):

        @pl.when(c != k)
        def _(k=k):
            send_g1(k).start()

        @pl.when(c == k)
        def _(k=k):
            g1_in[c] = g1_out[k]

    for q, dp in enumerate((dp0, dp1, dp2, dp3)):
        d_normed = d_normed + nt(dp, wp_ref[:, q * 128 : (q + 1) * 128])
    flat[...] = norm_backward(d_normed, zhat, zinv, ng_ref[...])
    for i in range(R):
        gpair_ref[i] = flat[i * K : (i + 1) * K].astype(BF16)

    for k in range(G):

        @pl.when(c != k)
        def _(k=k):
            copy(g1_out.at[k], g1_in.at[k], s_g1.at[k], r_g1.at[k], d, k).wait_recv()

    total = g1_in[0].astype(F32)
    for k in range(1, G):
        total = total + g1_in[k].astype(F32)
    g2_in[d] = total.astype(BF16)

    def send_g2(step):
        to = lax.rem(d + step, D)
        return copy(g2_in.at[d], g2_in.at[d], s_g2.at[step], r_g2.at[d], to, c)

    for step in range(1, D):
        send_g2(step).start()
    for step in range(1, D):
        frm = lax.rem(d + step, D)
        copy(g2_in.at[frm], g2_in.at[frm], s_g2.at[step], r_g2.at[frm], frm, c).wait_recv()
    total = g2_in[0].astype(F32)
    for k in range(1, D):
        total = total + g2_in[k].astype(F32)
    g3_in[c] = total.astype(BF16)

    def send_g3(step):
        to = lax.rem(c + step, G)
        return copy(g3_in.at[c], g3_in.at[c], s_g3.at[step], r_g3.at[c], d, to)

    for step in range(1, G):
        send_g3(step).start()

    for step in range(1, D):
        send_right(step).wait_send()

    @pl.when(c != home)
    def _():
        send_right(0).wait_send()

    for step in range(1, G):
        send_left(step).wait_send()
    for t in range(T):
        for k in range(G):

            @pl.when(jnp.logical_or(c * T + t != d, c != k))
            def _(t=t, k=k):
                send_dr(t, k).wait_send()

    for k in range(G):

        @pl.when(c != k)
        def _(k=k):
            send_dl(k).wait_send()
            send_g1(k).wait_send()

    for step in range(1, D):
        send_g2(step).wait_send()
    for step in range(1, G):
        frm = lax.rem(c + step, G)
        copy(g3_in.at[frm], g3_in.at[frm], s_g3.at[step], r_g3.at[frm], d, frm).wait_recv()
    for k in range(G):
        gproj_ref[k * S : (k + 1) * S] = g3_in[k].astype(F32)
    for step in range(1, G):
        send_g3(step).wait_send()


def local(sizes, pair, cotangent, mask, ng, nb, wp, wg, og, ob, wo):
    D, nchan, nsub = sizes
    R, K, C = pair.shape
    G = nchan * nsub
    N = K * G
    M = R * K
    T = K // R
    S = C // G
    vmem = pltpu.VMEM
    dma = pltpu.SemaphoreType.DMA
    scratch = [
        vmem((M, C), F32),
        vmem((M, C), F32),
        vmem((G, M, C), BF16),
        vmem((T * G, M, C), BF16),
        vmem((M, C), BF16),
        vmem((M, C), BF16),
        vmem((R, N, C), F32),
        vmem((K, N, C), F32),
        vmem((R, K, C), F32),
        vmem((R, K, C), F32),
        vmem((K, R, C), F32),
        vmem((R, N, C), F32),
        vmem((K, N, C), F32),
        vmem((M, C), F32),
        vmem((G, M, C), BF16),
        vmem((T * G, M, C), BF16),
        vmem((G, M, C), BF16),
        vmem((D, M, C), BF16),
        vmem((G, S, 4 * C), BF16),
        vmem((G, S, 4 * C), BF16),
        vmem((D, S, 4 * C), BF16),
        vmem((G, S, 4 * C), BF16),
        dma((D,)),
        dma((G,)),
        dma((T * G,)),
        dma((G,)),
        dma((G,)),
        dma((D,)),
        dma((G,)),
        dma((T * G,)),
        dma((G,)),
        dma((D,)),
        dma((G,)),
        dma((G,)),
        dma((D,)),
        dma((G,)),
    ]
    spec = pl.BlockSpec(memory_space=vmem)
    return pl.pallas_call(
        functools.partial(kernel, (R, K, D, G, nsub)),
        out_shape=(
            jax.ShapeDtypeStruct((R, K, C), BF16),
            jax.ShapeDtypeStruct((R, K, C), BF16),
            jax.ShapeDtypeStruct((C, 4 * C), F32),
        ),
        in_specs=[spec] * 10,
        out_specs=(spec,) * 3,
        scratch_shapes=scratch,
        compiler_params=pltpu.CompilerParams(
            collective_id=0,
            has_side_effects=True,
            vmem_limit_bytes=(16 if N * K <= 4096 else 56) * 1024 * 1024,
        ),
    )(
        pair,
        cotangent,
        mask.reshape(1, -1),
        ng.reshape(1, -1),
        nb.reshape(1, -1),
        wp,
        wg,
        og.reshape(1, -1),
        ob.reshape(1, -1),
        wo,
    )


def solution(mesh):
    block = P(("groups", "dap"), ("chan", "sub"), None)
    sizes = (mesh.shape["dap"], mesh.shape["chan"], mesh.shape["sub"])
    return jax.shard_map(
        functools.partial(local, sizes),
        mesh=mesh,
        in_specs=(block, block, P("groups")) + (P(),) * 7,
        out_specs=(block, block, P("groups", None)),
        check_vma=False,
    )
```

```python
import functools

import jax
import jax.numpy as jnp
from jax import lax
from jax.experimental import pallas as pl
from jax.experimental.pallas import tpu as pltpu
from jax.sharding import PartitionSpec as P

MESH = pl.DeviceIdType.MESH
F32 = jnp.float32
BF16 = jnp.bfloat16


def nn(a, b):
    return jnp.dot(a, b, preferred_element_type=F32)


def nt(a, b):
    return lax.dot_general(a, b, (((1,), (1,)), ((), ())), preferred_element_type=F32)


def tn(a, b):
    return lax.dot_general(a, b, (((0,), (0,)), ((), ())), preferred_element_type=F32)


def normalize(value):
    mean = jnp.mean(value, axis=1, keepdims=True)
    centred = value - mean
    inverse = lax.rsqrt(jnp.mean(centred * centred, axis=1, keepdims=True) + 1e-05)
    return centred * inverse, inverse


def norm_backward(incoming, normal, inverse, gain):
    scaled = incoming * gain
    return inverse * (
        scaled
        - jnp.mean(scaled, axis=1, keepdims=True)
        - normal * jnp.mean(scaled * normal, axis=1, keepdims=True)
    )


def kernel(
    dims,
    pair_hbm,
    cot_hbm,
    mask_hbm,
    ng_hbm,
    nb_hbm,
    wp_hbm,
    wg_hbm,
    og_hbm,
    ob_hbm,
    wo_hbm,
    update_ref,
    gpair_ref,
    gproj_ref,
    flat,
    flat2,
    left_in,
    right_in,
    own,
    left_all,
    right_all,
    left_n,
    right_n,
    cube,
    dm_row,
    dm_col,
    dl_all,
    dr_all,
    dpl,
    dpr,
    mcol,
    stage,
    dl_in,
    dr_in,
    grad,
    g1_out,
    g1_in,
    g2_in,
    g3_in,
    pair_ref,
    cot_ref,
    mask_ref,
    ng_ref,
    nb_ref,
    wp_ref,
    wg_ref,
    og_ref,
    ob_ref,
    wo_ref,
    s_in,
    s_right,
    s_left,
    s_dr,
    s_dl,
    s_g1,
    s_g2,
    s_g3,
    r_right,
    r_left,
    r_dr,
    r_dl,
    r_g1,
    r_g2,
    r_g3,
):
    R, K, D, G, nsub = dims
    N = K * G
    M = R * K
    T = K // R
    d = lax.axis_index("dap")
    c = lax.axis_index("chan") * nsub + lax.axis_index("sub")

    def at(dd, cc):
        return {"dap": dd, "chan": lax.div(cc, nsub), "sub": lax.rem(cc, nsub)}

    def copy(src, dst, send, recv, dd, cc):
        return pltpu.make_async_remote_copy(
            src_ref=src, dst_ref=dst, send_sem=send, recv_sem=recv,
            device_id=at(dd, cc), device_id_type=MESH,
        )

    ins = [
        pltpu.make_async_copy(src, dst, s_in.at[n])
        for n, (src, dst) in enumerate(
            (
                (pair_hbm, pair_ref),
                (ng_hbm, ng_ref),
                (nb_hbm, nb_ref),
                (mask_hbm, mask_ref),
                (wp_hbm, wp_ref),
                (wg_hbm, wg_ref),
                (cot_hbm, cot_ref),
                (og_hbm, og_ref),
                (ob_hbm, ob_ref),
                (wo_hbm, wo_ref),
            )
        )
    ]
    for one in ins:
        one.start()

    barrier = pltpu.get_barrier_semaphore()
    me = d * G + c

    def greet(step, carry):
        other = lax.rem(me + step, D * G)
        pl.semaphore_signal(
            barrier, inc=1, device_id=at(lax.div(other, G), lax.rem(other, G)), device_id_type=MESH
        )
        return carry

    lax.fori_loop(1, D * G, greet, 0)

    for one in ins[:3]:
        one.wait()
    for i in range(R):
        flat[i * K : (i + 1) * K] = pair_ref[i].astype(F32)
    zhat, zinv = normalize(flat[...])
    normed = (zhat * ng_ref[...] + nb_ref[...]).astype(BF16)
    own[...] = normed
    home = lax.div(d, T)
    part = lax.rem(d, T)
    pl.semaphore_wait(barrier, D * G - 1)

    def send_left(step):
        to = lax.rem(c + step, G)
        return copy(own, left_in.at[c], s_left.at[step], r_left.at[c], d, to)

    def send_right(step):
        to = lax.rem(d + step, D)
        slot = part * G + c
        return copy(own, right_in.at[slot], s_right.at[step], r_right.at[slot], to, home)

    for step in range(1, D):
        send_right(step).start()

    @pl.when(c != home)
    def _():
        send_right(0).start()

    for step in range(1, G):
        send_left(step).start()

    @pl.when(c == home)
    def _():
        right_in[part * G + c] = own[...]

    left_in[c] = own[...]

    for one in ins[3:]:
        one.wait()
    for i in range(R):
        flat2[i * K : (i + 1) * K] = cot_ref[i].astype(F32)
    maskf = mask_ref[...].astype(F32)
    here = lax.broadcasted_iota(jnp.int32, (N, N), 0)
    there = lax.broadcasted_iota(jnp.int32, (N, N), 1)
    mcol[...] = jnp.broadcast_to(
        jnp.sum(jnp.where(here == there, jnp.broadcast_to(maskf, (N, N)), 0.0), axis=1, keepdims=True),
        (N, 128),
    )
    row_at = lax.broadcasted_iota(jnp.int32, (M, N), 0)
    lane_at = lax.broadcasted_iota(jnp.int32, (M, N), 1)
    row_i = lax.div(row_at, K)
    row_k = row_at - row_i * K
    maskb = jnp.broadcast_to(maskf, (M, N))
    row_mask = jnp.sum(jnp.where(lane_at == row_i + d * R, maskb, 0.0), axis=1, keepdims=True)
    col_mask = jnp.sum(jnp.where(lane_at == row_k + c * K, maskb, 0.0), axis=1, keepdims=True)
    pmask = row_mask * col_mask
    left_val = nn(normed, wp_ref[:, 0:128])
    left_sig = jax.nn.sigmoid(nn(normed, wp_ref[:, 128:256]))
    right_val = nn(normed, wp_ref[:, 256:384])
    right_sig = jax.nn.sigmoid(nn(normed, wp_ref[:, 384:512]))
    left_scale = pmask * left_sig
    left_scale2 = left_scale * left_val * (1.0 - left_sig)
    right_scale = pmask * right_sig
    right_scale2 = right_scale * right_val * (1.0 - right_sig)
    gate = jax.nn.sigmoid(nn(normed, wg_ref[...]))
    upstream = flat2[...]

    group = max(g for g in range(1, R + 1) if R % g == 0 and (g == 1 or g * N <= 192))

    def edges(count, base, arrived, edge, sig, weights):
        def body(step, carry):
            at_row = pl.ds(step * group, group)
            rows = arrived[at_row].reshape(group * N, 128)
            proj = nn(rows, weights)
            gated = jax.nn.sigmoid(proj[:, 128:])
            value3 = (gated * proj[:, :128]).reshape(group, N, 128)
            gated3 = gated.reshape(group, N, 128)
            lane = lax.broadcasted_iota(jnp.int32, (1, N), 1)
            for g in range(group):
                present = jnp.sum(
                    jnp.where(lane == base + step * group + g, maskf, 0.0), axis=1, keepdims=True
                )
                masked = mcol[...] * present
                edge[step * group + g] = (masked * value3[g]).astype(BF16).astype(F32)
                sig[step * group + g] = gated3[g]
            return carry

        lax.fori_loop(0, count // group, body, 0)

    def get_left(step):
        frm = lax.rem(c + step, G)
        return copy(own, left_in.at[frm], s_left.at[step], r_left.at[frm], d, frm)

    for step in range(1, G):
        get_left(step).wait_recv()
    for k in range(G):
        stage[...] = left_in[k].astype(F32)
        for i in range(R):
            dl_all[i, k * K : (k + 1) * K] = stage[i * K : (i + 1) * K]
    for i in range(R):
        left_n[i] = dl_all[i].astype(BF16)
    edges(R, d * R, left_n, left_all, dl_all, wp_ref[:, 0:256])

    for t in range(T):
        for k in range(G):
            slot = t * G + k

            @pl.when(jnp.logical_or(c * T + t != d, c != k))
            def _(slot=slot, t=t, k=k):
                copy(
                    own, right_in.at[slot], s_right.at[0], r_right.at[slot], c * T + t, k
                ).wait_recv()

    for t in range(T):
        for k in range(G):
            stage[...] = right_in[t * G + k].astype(F32)
            for i in range(R):
                dr_all[t * R + i, k * K : (k + 1) * K] = stage[i * K : (i + 1) * K]
    for j in range(K):
        right_n[j] = dr_all[j].astype(BF16)
    edges(K, c * K, right_n, right_all, dr_all, wp_ref[:, 256:512])

    def mix_row(i, carry):
        row = left_all[i]
        for t in range(T):
            cube[i, t * R : (t + 1) * R] = jnp.sum(
                row[None] * right_all[t * R : (t + 1) * R], axis=1
            )
        return carry

    lax.fori_loop(0, R, mix_row, 0)
    for i in range(R):
        flat[i * K : (i + 1) * K] = cube[i]
    vhat, vinv = normalize(flat[...].astype(BF16).astype(F32))
    mixed_norm = (vhat * og_ref[...] + ob_ref[...]).astype(BF16)
    value = nn(mixed_norm, wo_ref[...])
    d_value = (upstream * gate).astype(BF16)
    d_mixed = norm_backward(nt(d_value, wo_ref[...]), vhat, vinv, og_ref[...])
    flat[...] = d_mixed.astype(BF16).astype(F32)
    for i in range(R):
        dm_row[i] = flat[i * K : (i + 1) * K]
    for j in range(K):
        dm_col[j] = flat[pl.ds(j, R, stride=K)]

    lanes = lax.broadcasted_iota(jnp.int32, (1, N), 1)

    def present(at_row):
        return jnp.sum(jnp.where(lanes == at_row, maskf, 0.0), axis=1, keepdims=True)

    chunk = 48 if N % 48 == 0 else N

    def dr_row(j, carry):
        weights = dm_col[j]
        for s in range(N // chunk):
            total = None
            for i in range(R):
                term = weights[i : i + 1] * left_all[i, s * chunk : (s + 1) * chunk]
                total = term if total is None else total + term
            cols = slice(s * chunk, (s + 1) * chunk)
            gated = dr_all[j, cols]
            dr_all[j, cols] = total
            masked = mcol[cols] * present(c * K + j)
            dpr[j, cols, 0:128] = (masked * gated * total).astype(BF16)
            dpr[j, cols, 128:256] = (right_all[j, cols] * (1.0 - gated) * total).astype(BF16)
        return carry

    lax.fori_loop(0, K, dr_row, 0)

    def send_dr(t, k):
        slot = t * G + k
        return copy(right_in.at[slot], dr_in.at[d], s_dr.at[slot], r_dr.at[d], c * T + t, k)

    for t in range(T):
        for k in range(G):
            slot = t * G + k
            for i in range(R):
                stage[i * K : (i + 1) * K] = dr_all[t * R + i, k * K : (k + 1) * K]
            right_in[slot] = stage[...].astype(BF16)
            mine = jnp.logical_and(c * T + t == d, c == k)

            @pl.when(jnp.logical_not(mine))
            def _(t=t, k=k):
                send_dr(t, k).start()

            @pl.when(mine)
            def _(slot=slot):
                dr_in[d] = right_in[slot]

    def dl_row(i, carry):
        weights = dm_row[i]
        for s in range(N // chunk):
            total = None
            for j in range(K):
                term = weights[j : j + 1] * right_all[j, s * chunk : (s + 1) * chunk]
                total = term if total is None else total + term
            cols = slice(s * chunk, (s + 1) * chunk)
            gated = dl_all[i, cols]
            dl_all[i, cols] = total
            masked = mcol[cols] * present(d * R + i)
            dpl[i, cols, 0:128] = (masked * gated * total).astype(BF16)
            dpl[i, cols, 128:256] = (left_all[i, cols] * (1.0 - gated) * total).astype(BF16)
        return carry

    lax.fori_loop(0, R, dl_row, 0)

    def send_dl(k):
        return copy(left_in.at[k], dl_in.at[c], s_dl.at[k], r_dl.at[c], d, k)

    for k in range(G):
        for i in range(R):
            stage[i * K : (i + 1) * K] = dl_all[i, k * K : (k + 1) * K]
        left_in[k] = stage[...].astype(BF16)

        @pl.when(c != k)
        def _(k=k):
            send_dl(k).start()

        @pl.when(c == k)
        def _(k=k):
            dl_in[c] = left_in[k]

    def add_grads(count, rows_ref, dp_ref, at_col):
        per = count if count * N <= 1024 else 1

        def term(step):
            at_row = pl.ds(step * per, per)
            return tn(
                rows_ref[at_row].reshape(per * N, 128), dp_ref[at_row].reshape(per * N, 256)
            )

        grad[:, at_col : at_col + 256] = term(0)
        if per < count:

            def body(step, carry):
                grad[:, at_col : at_col + 256] += term(step)
                return carry

            lax.fori_loop(1, count // per, body, 0)

    add_grads(K, right_n, dpr, 256)
    add_grads(R, left_n, dpl, 0)
    S = 128 // G
    for k in range(G):
        g1_out[k] = grad[k * S : (k + 1) * S].astype(BF16)

    def send_g1(k):
        return copy(g1_out.at[k], g1_in.at[c], s_g1.at[k], r_g1.at[c], d, k)

    for k in range(G):

        @pl.when(c != k)
        def _(k=k):
            send_g1(k).start()

        @pl.when(c == k)
        def _(k=k):
            g1_in[c] = g1_out[k]

    flat[...] = gate * value
    for i in range(R):
        update_ref[i] = flat[i * K : (i + 1) * K].astype(BF16)
    d_gate = (upstream * value * gate * (1.0 - gate)).astype(BF16)
    d_normed = nt(d_gate, wg_ref[...])
    for k in range(G):

        @pl.when(c != k)
        def _(k=k):
            copy(g1_out.at[k], g1_in.at[k], s_g1.at[k], r_g1.at[k], d, k).wait_recv()

    total = g1_in[0].astype(F32)
    for k in range(1, G):
        total = total + g1_in[k].astype(F32)
    g2_in[d] = total.astype(BF16)

    def send_g2(step):
        to = lax.rem(d + step, D)
        return copy(g2_in.at[d], g2_in.at[d], s_g2.at[step], r_g2.at[d], to, c)

    for step in range(1, D):
        send_g2(step).start()
    for step in range(1, D):
        frm = lax.rem(d + step, D)
        copy(g2_in.at[frm], g2_in.at[frm], s_g2.at[step], r_g2.at[frm], frm, c).wait_recv()
    total = g2_in[0].astype(F32)
    for k in range(1, D):
        total = total + g2_in[k].astype(F32)
    g3_in[c] = total.astype(BF16)

    def send_g3(step):
        to = lax.rem(c + step, G)
        return copy(g3_in.at[c], g3_in.at[c], s_g3.at[step], r_g3.at[c], d, to)

    for step in range(1, G):
        send_g3(step).start()

    for k in range(G):

        @pl.when(c != k)
        def _(k=k):
            copy(left_in.at[k], dl_in.at[k], s_dl.at[k], r_dl.at[k], d, k).wait_recv()

    d_left = dl_in[0].astype(F32)
    for k in range(1, G):
        d_left = d_left + dl_in[k].astype(F32)
    dp0 = (left_scale * d_left).astype(BF16)
    dp1 = (left_scale2 * d_left).astype(BF16)

    for k in range(D):

        @pl.when(jnp.logical_or(c != home, d != k))
        def _(k=k):
            copy(right_in.at[0], dr_in.at[k], s_dr.at[0], r_dr.at[k], k, home).wait_recv()

    d_right = dr_in[0].astype(F32)
    for k in range(1, D):
        d_right = d_right + dr_in[k].astype(F32)
    dp2 = (right_scale * d_right).astype(BF16)
    dp3 = (right_scale2 * d_right).astype(BF16)
    for q, dp in enumerate((dp0, dp1, dp2, dp3)):
        d_normed = d_normed + nt(dp, wp_ref[:, q * 128 : (q + 1) * 128])
    flat[...] = norm_backward(d_normed, zhat, zinv, ng_ref[...])
    for i in range(R):
        gpair_ref[i] = flat[i * K : (i + 1) * K].astype(BF16)

    for step in range(1, D):
        send_right(step).wait_send()

    @pl.when(c != home)
    def _():
        send_right(0).wait_send()

    for step in range(1, G):
        send_left(step).wait_send()
    for t in range(T):
        for k in range(G):

            @pl.when(jnp.logical_or(c * T + t != d, c != k))
            def _(t=t, k=k):
                send_dr(t, k).wait_send()

    for k in range(G):

        @pl.when(c != k)
        def _(k=k):
            send_dl(k).wait_send()
            send_g1(k).wait_send()

    for step in range(1, D):
        send_g2(step).wait_send()
    for step in range(1, G):
        frm = lax.rem(c + step, G)
        copy(g3_in.at[frm], g3_in.at[frm], s_g3.at[step], r_g3.at[frm], d, frm).wait_recv()
    for k in range(G):
        gproj_ref[k * S : (k + 1) * S] = g3_in[k].astype(F32)
    for step in range(1, G):
        send_g3(step).wait_send()


def local(sizes, pair, cotangent, mask, ng, nb, wp, wg, og, ob, wo):
    D, nchan, nsub = sizes
    R, K, C = pair.shape
    G = nchan * nsub
    N = K * G
    M = R * K
    T = K // R
    S = C // G
    vmem = pltpu.VMEM
    dma = pltpu.SemaphoreType.DMA
    scratch = [
        vmem((M, C), F32),
        vmem((M, C), F32),
        vmem((G, M, C), BF16),
        vmem((T * G, M, C), BF16),
        vmem((M, C), BF16),
        vmem((R, N, C), F32),
        vmem((K, N, C), F32),
        vmem((R, N, C), BF16),
        vmem((K, N, C), BF16),
        vmem((R, K, C), F32),
        vmem((R, K, C), F32),
        vmem((K, R, C), F32),
        vmem((R, N, C), F32),
        vmem((K, N, C), F32),
        vmem((R, N, 2 * C), BF16),
        vmem((K, N, 2 * C), BF16),
        vmem((N, C), F32),
        vmem((M, C), F32),
        vmem((G, M, C), BF16),
        vmem((D, M, C), BF16),
        vmem((C, 4 * C), F32),
        vmem((G, S, 4 * C), BF16),
        vmem((G, S, 4 * C), BF16),
        vmem((D, S, 4 * C), BF16),
        vmem((G, S, 4 * C), BF16),
        vmem((R, K, C), BF16),
        vmem((R, K, C), BF16),
        vmem((1, N), jnp.int32),
        vmem((1, C), F32),
        vmem((1, C), F32),
        vmem((C, 4 * C), BF16),
        vmem((C, C), BF16),
        vmem((1, C), F32),
        vmem((1, C), F32),
        vmem((C, C), BF16),
        dma((10,)),
        dma((D,)),
        dma((G,)),
        dma((T * G,)),
        dma((G,)),
        dma((G,)),
        dma((D,)),
        dma((G,)),
        dma((T * G,)),
        dma((G,)),
        dma((D,)),
        dma((G,)),
        dma((G,)),
        dma((D,)),
        dma((G,)),
    ]
    spec = pl.BlockSpec(memory_space=vmem)
    return pl.pallas_call(
        functools.partial(kernel, (R, K, D, G, nsub)),
        out_shape=(
            jax.ShapeDtypeStruct((R, K, C), BF16),
            jax.ShapeDtypeStruct((R, K, C), BF16),
            jax.ShapeDtypeStruct((C, 4 * C), F32),
        ),
        in_specs=[pl.BlockSpec(memory_space=pltpu.HBM)] * 10,
        out_specs=(spec,) * 3,
        scratch_shapes=scratch,
        compiler_params=pltpu.CompilerParams(
            collective_id=0,
            has_side_effects=True,
            vmem_limit_bytes=60 * 1024 * 1024,
        ),
    )(
        pair,
        cotangent,
        mask.reshape(1, -1),
        ng.reshape(1, -1),
        nb.reshape(1, -1),
        wp,
        wg,
        og.reshape(1, -1),
        ob.reshape(1, -1),
        wo,
    )


def solution(mesh):
    block = P(("groups", "dap"), ("chan", "sub"), None)
    sizes = (mesh.shape["dap"], mesh.shape["chan"], mesh.shape["sub"])
    return jax.shard_map(
        functools.partial(local, sizes),
        mesh=mesh,
        in_specs=(block, block, P("groups")) + (P(),) * 7,
        out_specs=(block, block, P("groups", None)),
        check_vma=False,
    )
```

```python
import functools

import jax
import jax.numpy as jnp
from jax import lax
from jax.experimental import pallas as pl
from jax.experimental.pallas import tpu as pltpu
from jax.sharding import PartitionSpec as P

MESH = pl.DeviceIdType.MESH
F32 = jnp.float32
BF16 = jnp.bfloat16


def nn(a, b):
    return jnp.dot(a, b, preferred_element_type=F32)


def nt(a, b):
    return lax.dot_general(a, b, (((1,), (1,)), ((), ())), preferred_element_type=F32)


def tn(a, b):
    return lax.dot_general(a, b, (((0,), (0,)), ((), ())), preferred_element_type=F32)


def normalize(value):
    mean = jnp.mean(value, axis=1, keepdims=True)
    centred = value - mean
    inverse = lax.rsqrt(jnp.mean(centred * centred, axis=1, keepdims=True) + 1e-05)
    return centred * inverse, inverse


def norm_backward(incoming, normal, inverse, gain):
    scaled = incoming * gain
    return inverse * (
        scaled
        - jnp.mean(scaled, axis=1, keepdims=True)
        - normal * jnp.mean(scaled * normal, axis=1, keepdims=True)
    )


def kernel(
    dims,
    pair_hbm,
    cot_hbm,
    mask_hbm,
    ng_hbm,
    nb_hbm,
    wp_hbm,
    wg_hbm,
    og_hbm,
    ob_hbm,
    wo_hbm,
    update_ref,
    gpair_ref,
    gproj_ref,
    flat,
    flat2,
    left_in,
    right_in,
    own,
    left_all,
    right_all,
    left_n,
    right_n,
    cube,
    dm_row,
    dm_col,
    dl_all,
    dr_all,
    dpl,
    dpr,
    mcol,
    stage,
    dl_in,
    dr_in,
    grad,
    g1_out,
    g1_in,
    g2_in,
    g3_in,
    pair_ref,
    cot_ref,
    mask_ref,
    ng_ref,
    nb_ref,
    wp_ref,
    wg_ref,
    og_ref,
    ob_ref,
    wo_ref,
    s_in,
    s_right,
    s_left,
    s_dr,
    s_dl,
    s_g1,
    s_g2,
    s_g3,
    r_right,
    r_left,
    r_dr,
    r_dl,
    r_g1,
    r_g2,
    r_g3,
):
    R, K, D, G, nsub = dims
    N = K * G
    M = R * K
    T = K // R
    d = lax.axis_index("dap")
    c = lax.axis_index("chan") * nsub + lax.axis_index("sub")

    def at(dd, cc):
        return {"dap": dd, "chan": lax.div(cc, nsub), "sub": lax.rem(cc, nsub)}

    def copy(src, dst, send, recv, dd, cc):
        return pltpu.make_async_remote_copy(
            src_ref=src, dst_ref=dst, send_sem=send, recv_sem=recv,
            device_id=at(dd, cc), device_id_type=MESH,
        )

    ins = [
        pltpu.make_async_copy(src, dst, s_in.at[n])
        for n, (src, dst) in enumerate(
            (
                (pair_hbm, pair_ref),
                (ng_hbm, ng_ref),
                (nb_hbm, nb_ref),
                (mask_hbm, mask_ref),
                (wp_hbm, wp_ref),
                (wg_hbm, wg_ref),
                (cot_hbm, cot_ref),
                (og_hbm, og_ref),
                (ob_hbm, ob_ref),
                (wo_hbm, wo_ref),
            )
        )
    ]
    for one in ins:
        one.start()

    barrier = pltpu.get_barrier_semaphore()
    me = d * G + c

    def greet(step, carry):
        other = lax.rem(me + step, D * G)
        pl.semaphore_signal(
            barrier, inc=1, device_id=at(lax.div(other, G), lax.rem(other, G)), device_id_type=MESH
        )
        return carry

    lax.fori_loop(1, D * G, greet, 0)

    for one in ins[:3]:
        one.wait()
    for i in range(R):
        flat[i * K : (i + 1) * K] = pair_ref[i].astype(F32)
    zhat, zinv = normalize(flat[...])
    normed = (zhat * ng_ref[...] + nb_ref[...]).astype(BF16)
    own[...] = normed
    home = lax.div(d, T)
    part = lax.rem(d, T)
    pl.semaphore_wait(barrier, D * G - 1)

    def send_left(step):
        to = lax.rem(c + step, G)
        return copy(own, left_in.at[c], s_left.at[step], r_left.at[c], d, to)

    def send_right(step):
        to = lax.rem(d + step, D)
        slot = part * G + c
        return copy(own, right_in.at[slot], s_right.at[step], r_right.at[slot], to, home)

    for step in range(1, D):
        send_right(step).start()

    @pl.when(c != home)
    def _():
        send_right(0).start()

    for step in range(1, G):
        send_left(step).start()

    @pl.when(c == home)
    def _():
        right_in[part * G + c] = own[...]

    left_in[c] = own[...]

    for one in ins[3:]:
        one.wait()
    for i in range(R):
        flat2[i * K : (i + 1) * K] = cot_ref[i].astype(F32)
    maskf = mask_ref[...].astype(F32)
    here = lax.broadcasted_iota(jnp.int32, (N, N), 0)
    there = lax.broadcasted_iota(jnp.int32, (N, N), 1)
    mcol[...] = jnp.broadcast_to(
        jnp.sum(jnp.where(here == there, jnp.broadcast_to(maskf, (N, N)), 0.0), axis=1, keepdims=True),
        (N, 128),
    )
    row_at = lax.broadcasted_iota(jnp.int32, (M, N), 0)
    lane_at = lax.broadcasted_iota(jnp.int32, (M, N), 1)
    row_i = lax.div(row_at, K)
    row_k = row_at - row_i * K
    maskb = jnp.broadcast_to(maskf, (M, N))
    row_mask = jnp.sum(jnp.where(lane_at == row_i + d * R, maskb, 0.0), axis=1, keepdims=True)
    col_mask = jnp.sum(jnp.where(lane_at == row_k + c * K, maskb, 0.0), axis=1, keepdims=True)
    pmask = row_mask * col_mask
    left_val = nn(normed, wp_ref[:, 0:128])
    left_sig = jax.nn.sigmoid(nn(normed, wp_ref[:, 128:256]))
    right_val = nn(normed, wp_ref[:, 256:384])
    right_sig = jax.nn.sigmoid(nn(normed, wp_ref[:, 384:512]))
    left_scale = pmask * left_sig
    left_scale2 = left_scale * left_val * (1.0 - left_sig)
    right_scale = pmask * right_sig
    right_scale2 = right_scale * right_val * (1.0 - right_sig)
    gate = jax.nn.sigmoid(nn(normed, wg_ref[...]))
    upstream = flat2[...]

    group = max(g for g in range(1, R + 1) if R % g == 0 and (g == 1 or g * N <= 192))

    def edges(count, base, arrived, edge, sig, weights):
        def body(step, carry):
            at_row = pl.ds(step * group, group)
            rows = arrived[at_row].reshape(group * N, 128)
            proj = nn(rows, weights)
            gated = jax.nn.sigmoid(proj[:, 128:])
            value3 = (gated * proj[:, :128]).reshape(group, N, 128)
            gated3 = gated.reshape(group, N, 128)
            lane = lax.broadcasted_iota(jnp.int32, (1, N), 1)
            for g in range(group):
                present = jnp.sum(
                    jnp.where(lane == base + step * group + g, maskf, 0.0), axis=1, keepdims=True
                )
                masked = mcol[...] * present
                edge[step * group + g] = (masked * value3[g]).astype(BF16).astype(F32)
                sig[step * group + g] = gated3[g]
            return carry

        lax.fori_loop(0, count // group, body, 0)

    def get_left(step):
        frm = lax.rem(c + step, G)
        return copy(own, left_in.at[frm], s_left.at[step], r_left.at[frm], d, frm)

    for step in range(1, G):
        get_left(step).wait_recv()
    for k in range(G):
        stage[...] = left_in[k].astype(F32)
        for i in range(R):
            dl_all[i, k * K : (k + 1) * K] = stage[i * K : (i + 1) * K]
    for i in range(R):
        left_n[i] = dl_all[i].astype(BF16)
    edges(R, d * R, left_n, left_all, dl_all, wp_ref[:, 0:256])

    for t in range(T):
        for k in range(G):
            slot = t * G + k

            @pl.when(jnp.logical_or(c * T + t != d, c != k))
            def _(slot=slot, t=t, k=k):
                copy(
                    own, right_in.at[slot], s_right.at[0], r_right.at[slot], c * T + t, k
                ).wait_recv()

    for t in range(T):
        for k in range(G):
            stage[...] = right_in[t * G + k].astype(F32)
            for i in range(R):
                dr_all[t * R + i, k * K : (k + 1) * K] = stage[i * K : (i + 1) * K]
    for j in range(K):
        right_n[j] = dr_all[j].astype(BF16)
    edges(K, c * K, right_n, right_all, dr_all, wp_ref[:, 256:512])

    def mix_row(i, carry):
        row = left_all[i]
        for t in range(T):
            cube[i, t * R : (t + 1) * R] = jnp.sum(
                row[None] * right_all[t * R : (t + 1) * R], axis=1
            )
        return carry

    lax.fori_loop(0, R, mix_row, 0)
    for i in range(R):
        flat[i * K : (i + 1) * K] = cube[i]
    vhat, vinv = normalize(flat[...].astype(BF16).astype(F32))
    mixed_norm = (vhat * og_ref[...] + ob_ref[...]).astype(BF16)
    value = nn(mixed_norm, wo_ref[...])
    d_value = (upstream * gate).astype(BF16)
    d_mixed = norm_backward(nt(d_value, wo_ref[...]), vhat, vinv, og_ref[...])
    flat[...] = d_mixed.astype(BF16).astype(F32)
    for i in range(R):
        dm_row[i] = flat[i * K : (i + 1) * K]
    for j in range(K):
        dm_col[j] = flat[pl.ds(j, R, stride=K)]

    lanes = lax.broadcasted_iota(jnp.int32, (1, N), 1)

    def present(at_row):
        return jnp.sum(jnp.where(lanes == at_row, maskf, 0.0), axis=1, keepdims=True)

    chunk = 48 if N % 48 == 0 else N

    def dr_row(j, carry):
        weights = dm_col[j]
        for s in range(N // chunk):
            total = None
            for i in range(R):
                term = weights[i : i + 1] * left_all[i, s * chunk : (s + 1) * chunk]
                total = term if total is None else total + term
            cols = slice(s * chunk, (s + 1) * chunk)
            gated = dr_all[j, cols]
            dr_all[j, cols] = total
            masked = mcol[cols] * present(c * K + j)
            dpr[j, cols, 0:128] = (masked * gated * total).astype(BF16)
            dpr[j, cols, 128:256] = (right_all[j, cols] * (1.0 - gated) * total).astype(BF16)
        return carry

    lax.fori_loop(0, K, dr_row, 0)

    def send_dr(t, k):
        slot = t * G + k
        return copy(right_in.at[slot], dr_in.at[d], s_dr.at[slot], r_dr.at[d], c * T + t, k)

    for t in range(T):
        for k in range(G):
            slot = t * G + k
            for i in range(R):
                stage[i * K : (i + 1) * K] = dr_all[t * R + i, k * K : (k + 1) * K]
            right_in[slot] = stage[...].astype(BF16)
            mine = jnp.logical_and(c * T + t == d, c == k)

            @pl.when(jnp.logical_not(mine))
            def _(t=t, k=k):
                send_dr(t, k).start()

            @pl.when(mine)
            def _(slot=slot):
                dr_in[d] = right_in[slot]

    def dl_row(i, carry):
        weights = dm_row[i]
        for s in range(N // chunk):
            total = None
            for j in range(K):
                term = weights[j : j + 1] * right_all[j, s * chunk : (s + 1) * chunk]
                total = term if total is None else total + term
            cols = slice(s * chunk, (s + 1) * chunk)
            gated = dl_all[i, cols]
            dl_all[i, cols] = total
            masked = mcol[cols] * present(d * R + i)
            dpl[i, cols, 0:128] = (masked * gated * total).astype(BF16)
            dpl[i, cols, 128:256] = (left_all[i, cols] * (1.0 - gated) * total).astype(BF16)
        return carry

    lax.fori_loop(0, R, dl_row, 0)

    def send_dl(k):
        return copy(left_in.at[k], dl_in.at[c], s_dl.at[k], r_dl.at[c], d, k)

    for k in range(G):
        for i in range(R):
            stage[i * K : (i + 1) * K] = dl_all[i, k * K : (k + 1) * K]
        left_in[k] = stage[...].astype(BF16)

        @pl.when(c != k)
        def _(k=k):
            send_dl(k).start()

        @pl.when(c == k)
        def _(k=k):
            dl_in[c] = left_in[k]

    def add_grads(count, rows_ref, dp_ref, at_col):
        per = count if count * N <= 1024 else 1

        def term(step):
            at_row = pl.ds(step * per, per)
            return tn(
                rows_ref[at_row].reshape(per * N, 128), dp_ref[at_row].reshape(per * N, 256)
            )

        grad[:, at_col : at_col + 256] = term(0)
        if per < count:

            def body(step, carry):
                grad[:, at_col : at_col + 256] += term(step)
                return carry

            lax.fori_loop(1, count // per, body, 0)

    add_grads(K, right_n, dpr, 256)
    add_grads(R, left_n, dpl, 0)
    S = 128 // G
    for k in range(G):
        g1_out[k] = grad[k * S : (k + 1) * S].astype(BF16)

    def send_g1(k):
        return copy(g1_out.at[k], g1_in.at[c], s_g1.at[k], r_g1.at[c], d, k)

    for k in range(G):

        @pl.when(c != k)
        def _(k=k):
            send_g1(k).start()

        @pl.when(c == k)
        def _(k=k):
            g1_in[c] = g1_out[k]

    flat[...] = gate * value
    for i in range(R):
        update_ref[i] = flat[i * K : (i + 1) * K].astype(BF16)
    d_gate = (upstream * value * gate * (1.0 - gate)).astype(BF16)
    d_normed = nt(d_gate, wg_ref[...])
    for k in range(G):

        @pl.when(c != k)
        def _(k=k):
            copy(g1_out.at[k], g1_in.at[k], s_g1.at[k], r_g1.at[k], d, k).wait_recv()

    total = g1_in[0].astype(F32)
    for k in range(1, G):
        total = total + g1_in[k].astype(F32)
    g2_in[d] = total.astype(BF16)

    def send_g2(step):
        to = lax.rem(d + step, D)
        return copy(g2_in.at[d], g2_in.at[d], s_g2.at[step], r_g2.at[d], to, c)

    for step in range(1, D):
        send_g2(step).start()
    for step in range(1, D):
        frm = lax.rem(d + step, D)
        copy(g2_in.at[frm], g2_in.at[frm], s_g2.at[step], r_g2.at[frm], frm, c).wait_recv()
    total = g2_in[0].astype(F32)
    for k in range(1, D):
        total = total + g2_in[k].astype(F32)
    g3_in[c] = total.astype(BF16)

    def send_g3(step):
        to = lax.rem(c + step, G)
        return copy(g3_in.at[c], g3_in.at[c], s_g3.at[step], r_g3.at[c], d, to)

    for step in range(1, G):
        send_g3(step).start()

    for k in range(G):

        @pl.when(c != k)
        def _(k=k):
            copy(left_in.at[k], dl_in.at[k], s_dl.at[k], r_dl.at[k], d, k).wait_recv()

    d_left = dl_in[0].astype(F32)
    for k in range(1, G):
        d_left = d_left + dl_in[k].astype(F32)
    dp0 = (left_scale * d_left).astype(BF16)
    dp1 = (left_scale2 * d_left).astype(BF16)

    for k in range(D):

        @pl.when(jnp.logical_or(c != home, d != k))
        def _(k=k):
            copy(right_in.at[0], dr_in.at[k], s_dr.at[0], r_dr.at[k], k, home).wait_recv()

    d_right = dr_in[0].astype(F32)
    for k in range(1, D):
        d_right = d_right + dr_in[k].astype(F32)
    dp2 = (right_scale * d_right).astype(BF16)
    dp3 = (right_scale2 * d_right).astype(BF16)
    for q, dp in enumerate((dp0, dp1, dp2, dp3)):
        d_normed = d_normed + nt(dp, wp_ref[:, q * 128 : (q + 1) * 128])
    flat[...] = norm_backward(d_normed, zhat, zinv, ng_ref[...])
    for i in range(R):
        gpair_ref[i] = flat[i * K : (i + 1) * K].astype(BF16)

    for step in range(1, D):
        send_right(step).wait_send()

    @pl.when(c != home)
    def _():
        send_right(0).wait_send()

    for step in range(1, G):
        send_left(step).wait_send()
    for t in range(T):
        for k in range(G):

            @pl.when(jnp.logical_or(c * T + t != d, c != k))
            def _(t=t, k=k):
                send_dr(t, k).wait_send()

    for k in range(G):

        @pl.when(c != k)
        def _(k=k):
            send_dl(k).wait_send()
            send_g1(k).wait_send()

    for step in range(1, D):
        send_g2(step).wait_send()
    for step in range(1, G):
        frm = lax.rem(c + step, G)
        copy(g3_in.at[frm], g3_in.at[frm], s_g3.at[step], r_g3.at[frm], d, frm).wait_recv()
    for k in range(G):
        gproj_ref[k * S : (k + 1) * S] = g3_in[k].astype(F32)
    for step in range(1, G):
        send_g3(step).wait_send()


def write_out(a, b, c, a_out, b_out, c_out, sems):
    copies = [
        pltpu.make_async_copy(src, dst, sems.at[n])
        for n, (src, dst) in enumerate(((c, c_out), (a, a_out), (b, b_out)))
    ]
    for one in copies:
        one.start()
    for one in copies:
        one.wait()


def local(sizes, pair, cotangent, mask, ng, nb, wp, wg, og, ob, wo):
    D, nchan, nsub = sizes
    R, K, C = pair.shape
    G = nchan * nsub
    N = K * G
    M = R * K
    T = K // R
    S = C // G
    vmem = pltpu.VMEM
    dma = pltpu.SemaphoreType.DMA
    scratch = [
        vmem((M, C), F32),
        vmem((M, C), F32),
        vmem((G, M, C), BF16),
        vmem((T * G, M, C), BF16),
        vmem((M, C), BF16),
        vmem((R, N, C), F32),
        vmem((K, N, C), F32),
        vmem((R, N, C), BF16),
        vmem((K, N, C), BF16),
        vmem((R, K, C), F32),
        vmem((R, K, C), F32),
        vmem((K, R, C), F32),
        vmem((R, N, C), F32),
        vmem((K, N, C), F32),
        vmem((R, N, 2 * C), BF16),
        vmem((K, N, 2 * C), BF16),
        vmem((N, C), F32),
        vmem((M, C), F32),
        vmem((G, M, C), BF16),
        vmem((D, M, C), BF16),
        vmem((C, 4 * C), F32),
        vmem((G, S, 4 * C), BF16),
        vmem((G, S, 4 * C), BF16),
        vmem((D, S, 4 * C), BF16),
        vmem((G, S, 4 * C), BF16),
        vmem((R, K, C), BF16),
        vmem((R, K, C), BF16),
        vmem((1, N), jnp.int32),
        vmem((1, C), F32),
        vmem((1, C), F32),
        vmem((C, 4 * C), BF16),
        vmem((C, C), BF16),
        vmem((1, C), F32),
        vmem((1, C), F32),
        vmem((C, C), BF16),
        dma((10,)),
        dma((D,)),
        dma((G,)),
        dma((T * G,)),
        dma((G,)),
        dma((G,)),
        dma((D,)),
        dma((G,)),
        dma((T * G,)),
        dma((G,)),
        dma((D,)),
        dma((G,)),
        dma((G,)),
        dma((D,)),
        dma((G,)),
    ]
    spec = pl.BlockSpec(memory_space=vmem)
    results = pl.pallas_call(
        functools.partial(kernel, (R, K, D, G, nsub)),
        out_shape=(
            vmem((R, K, C), BF16),
            vmem((R, K, C), BF16),
            vmem((C, 4 * C), F32),
        ),
        in_specs=[pl.BlockSpec(memory_space=pltpu.HBM)] * 10,
        out_specs=(spec,) * 3,
        scratch_shapes=scratch,
        compiler_params=pltpu.CompilerParams(
            collective_id=0,
            has_side_effects=True,
            vmem_limit_bytes=60 * 1024 * 1024,
        ),
    )(
        pair,
        cotangent,
        mask.reshape(1, -1),
        ng.reshape(1, -1),
        nb.reshape(1, -1),
        wp,
        wg,
        og.reshape(1, -1),
        ob.reshape(1, -1),
        wo,
    )

    return pl.pallas_call(
        write_out,
        out_shape=tuple(jax.ShapeDtypeStruct(r.shape, r.dtype) for r in results),
        in_specs=[pl.BlockSpec(memory_space=pl.ANY)] * 3,
        out_specs=(pl.BlockSpec(memory_space=pl.ANY),) * 3,
        scratch_shapes=[dma((3,))],
        compiler_params=pltpu.CompilerParams(vmem_limit_bytes=1024 * 1024),
    )(*results)


def solution(mesh):
    block = P(("groups", "dap"), ("chan", "sub"), None)
    sizes = (mesh.shape["dap"], mesh.shape["chan"], mesh.shape["sub"])
    return jax.shard_map(
        functools.partial(local, sizes),
        mesh=mesh,
        in_specs=(block, block, P("groups")) + (P(),) * 7,
        out_specs=(block, block, P("groups", None)),
        check_vma=False,
    )
```
